256 devices in a mesh: section: 16 (over z_lo, x, core), expert: 16 (over y, z_hi).
Axes of the slice: x: 4, y: 4, z: 8 (z_hi: 4, z_lo: 2; z = z_hi * 2 + z_lo), core: 2. Of those that a mesh axis runs over, the one named last changes fastest.
Arguments:
- handoff: bfloat16 [16, 2048, 2560], P('section', 'expert'), may hold values from -6 to 6
- grad_handoff: bfloat16 [16, 2048, 2560], P('section', 'expert'), may hold values from -6 to 6
- parked: bfloat16 [16, 2048, 2560], P('section', 'expert'), may hold values from -6 to 6
- ids_fwd: int32 [16, 2048, 2], P('section', 'expert'), may hold values from 0 to 7, all different within a row; in each aligned block of 128 rows (0 to 127, 128 to 255, ..., all dimensions but the last counted through in order) at most 48 rows name the same one
- gates_fwd: float32 [16, 2048, 2], P('section', 'expert'), may hold values from 0.2 to 1
- ids_bwd: int32 [16, 2048, 2], P('section', 'expert'), may hold values from 0 to 7, all different within a row; in each aligned block of 128 rows (0 to 127, 128 to 255, ..., all dimensions but the last counted through in order) at most 48 rows name the same one
- gates_bwd: float32 [16, 2048, 2], P('section', 'expert'), may hold values from 0.2 to 1
- w_gate: bfloat16 [16, 16, 2560, 384], P('section', 'expert'), may hold values from -0.125 to 0.125
- w_up: bfloat16 [16, 16, 2560, 384], P('section', 'expert'), may hold values from -0.125 to 0.125
- w_down: bfloat16 [16, 16, 384, 2560], P('section', 'expert'), may hold values from -0.21875 to 0.21875
Outputs:
- forward_out: bfloat16 [16, 2048, 2560], P('section', 'expert')
- backward_out: bfloat16 [16, 2048, 2560], P('section', 'expert')
The draws below stay inside these ranges and needn't reach their ends.
Inputs may be any that keep to these rules, and one draw needn't show every extreme that they name: `ids_fwd`: the 2 ids of a token differ. Among the 128 tokens of one device, no expert is chosen by more than 48, and some expert is chosen by exactly 48 in some device's tokens. `ids_bwd`: as ids_fwd.
All inputs are finite; a program needn't handle non-finite values.
Results may differ from the reference program's by a relative error of at most 0.014.
Values may be sent and summed in bfloat16 or wider, within the bound.
A program may use at most 128 MiB of HBM per device.

```python
import math
import jax
import jax.numpy as jnp
import numpy as np
from jax import lax

D = 2560
FFE = 768
EXPERTS = 8
TOP = 2
TOK_DEV = 128
CAP = 48
SPLIT = 2
H_DEV = 384
TOKENS = 2048
SECTIONS = 16
N_EXPERT = 16


def level_of(key, dims, shards, low, high):
    def one(dim, shards_of):
        heights = jax.random.uniform(jax.random.fold_in(jax.random.fold_in(key, 6), dim), (shards_of,), jnp.float32, low / len(shards), high / len(shards))
        return jnp.repeat(jnp.exp(heights), dims[dim] // shards_of).reshape((-1,) + (1,) * (len(dims) - dim - 1))

    gain = one(*shards[0])
    for cut in shards[1:]:
        gain = gain * one(*cut)
    return gain


def assign_block(stream_key, own, number, rows, number_of, top, bound, slope):
    ranking = jax.random.permutation(stream_key, number_of)
    heavy_load, ordinary = shares(number_of, rows * top, bound, slope, True), shares(number_of, rows * top, bound, slope, False)
    places = jnp.arange(number_of)

    def named(lengths, rotation):
        used = int((lengths > 0).sum())
        fixed = max(1, used // 4)
        moved = fixed + (places - fixed + rotation * (used - fixed)) % max(1, number_of - fixed)
        return jnp.zeros((number_of,), jnp.int32).at[ranking[jnp.where(places < fixed, places, moved)]].set(jnp.asarray(lengths, jnp.int32))

    lengths = jnp.where(number % 4 == 0, named(heavy_load, number // 4), named(ordinary, number - number // 4 - 1))
    mixed = jax.random.permutation(jax.random.fold_in(own, 3), number_of)
    donor, sink = mixed[0:number_of // 2 * 2:2], mixed[1:number_of // 2 * 2:2]
    slack = jnp.minimum(lengths[donor] - 1, bound - lengths[sink]) // 2
    slack = jnp.where((donor == ranking[0]) | (sink == ranking[0]) | (lengths[sink] == 0), 0, jnp.maximum(slack, 0))
    moved = jax.random.randint(jax.random.fold_in(own, 4), (number_of // 2,), 0, 1 << 20) % (slack + 1)
    lengths = lengths.at[donor].add(-moved).at[sink].add(moved)
    labels = jnp.searchsorted(jnp.cumsum(lengths), jnp.arange(rows * top), side="right").astype(jnp.int32)
    table = labels.reshape(top, rows).T
    table = table[jax.random.permutation(jax.random.fold_in(own, 1), rows)]
    rotation = jax.random.randint(jax.random.fold_in(own, 2), (rows, 1), 0, top)
    return jnp.take_along_axis(table, (jnp.arange(top)[None, :] + rotation) % top, axis=1)


def shares(count, total, limit, lean, full):
    loads = [(1 << 20) // math.isqrt(rank ** lean) + 1 for rank in range(1, count + 1)]
    largest = limit if full else min(limit, max(-(-total // count), total * loads[0] // sum(loads)))
    least = 1 if total - largest >= count - 1 else 0
    counts, spare = [largest] + [least] * (count - 1), total - largest - least * (count - 1)
    while spare > 0:
        candidates = [i for i in range(1, count) if counts[i] < largest] or [i for i in range(1, count) if counts[i] < limit]
        whole, remaining = sum([loads[i] for i in candidates]), spare
        for i in candidates:
            more = min(limit - counts[i], max(1, remaining * loads[i] // whole), spare)
            counts[i] = counts[i] + more
            spare = spare - more
    return np.array(counts)


def noise(key, shape, deviation, reach, shards=(), kind=jnp.bfloat16):
    values = jax.random.normal(key, shape, jnp.float32) * deviation
    if len(shards) > 0:
        values = level_of(key, shape, shards, -0.22, 0.18) * values
    return jnp.clip(values, min=-reach, max=reach).astype(kind)


def setup_inputs(seed: int = 0) -> dict:
    streams_of = jax.random.split(jax.random.key(seed), 11)
    handoff = noise(streams_of[0], (SECTIONS, TOKENS, D), 1.0, 6.0, ((0, 16), (1, 16)))
    grad_handoff = noise(streams_of[1], (SECTIONS, TOKENS, D), 1.0, 6.0, ((0, 16), (1, 16)))
    parked = noise(streams_of[2], (SECTIONS, TOKENS, D), 1.0, 6.0, ((0, 16), (1, 16)))
    ids_fwd_keys = jax.random.split(jax.random.fold_in(streams_of[3], 1), SECTIONS * TOKENS // TOK_DEV)
    ids_fwd_turns = jax.random.permutation(jax.random.fold_in(streams_of[3], 3), SECTIONS * TOKENS // TOK_DEV)
    ids_fwd = jax.vmap(lambda own, number: assign_block(jax.random.fold_in(streams_of[3], 2), own, number, TOK_DEV, EXPERTS, TOP, CAP, 2))(ids_fwd_keys, ids_fwd_turns).reshape((SECTIONS, TOKENS, TOP))
    gates_fwd = jnp.clip(0.2 + 0.8 * jax.random.uniform(streams_of[4], (SECTIONS, TOKENS, TOP), jnp.float32) ** level_of(streams_of[4], (SECTIONS, TOKENS, TOP), ((0, 16), (1, 16)), -0.2, 0.2), 0.2, 1.0)
    ids_bwd_keys = jax.random.split(jax.random.fold_in(streams_of[5], 1), SECTIONS * TOKENS // TOK_DEV)
    ids_bwd_turns = jax.random.permutation(jax.random.fold_in(streams_of[5], 3), SECTIONS * TOKENS // TOK_DEV)
    ids_bwd = jax.vmap(lambda own, number: assign_block(jax.random.fold_in(streams_of[5], 2), own, number, TOK_DEV, EXPERTS, TOP, CAP, 2))(ids_bwd_keys, ids_bwd_turns).reshape((SECTIONS, TOKENS, TOP))
    gates_bwd = jnp.clip(0.2 + 0.8 * jax.random.uniform(streams_of[6], (SECTIONS, TOKENS, TOP), jnp.float32) ** level_of(streams_of[6], (SECTIONS, TOKENS, TOP), ((0, 16), (1, 16)), -0.2, 0.2), 0.2, 1.0)
    w_gate = noise(streams_of[7], (SECTIONS, EXPERTS * SPLIT, D, H_DEV), D ** -0.5, 0.125, ((0, 16), (1, 16)))
    w_up = noise(streams_of[8], (SECTIONS, EXPERTS * SPLIT, D, H_DEV), D ** -0.5, 0.125, ((0, 16), (1, 16)))
    w_down = noise(streams_of[9], (SECTIONS, EXPERTS * SPLIT, H_DEV, D), FFE ** -0.5, 0.21875, ((0, 16), (1, 16)))
    return {"handoff": handoff, "grad_handoff": grad_handoff, "parked": parked, "ids_fwd": ids_fwd, "gates_fwd": gates_fwd, "ids_bwd": ids_bwd, "gates_bwd": gates_bwd, "w_gate": w_gate, "w_up": w_up, "w_down": w_down}


def slot_index(expert_ids, expert_count, per_expert):
    flat_ids = expert_ids.reshape(-1).astype(jnp.int32)
    onehot = (flat_ids[:, None] == jnp.arange(expert_count, dtype=jnp.int32)[None, :]).astype(jnp.int32)
    before = jnp.cumsum(onehot, axis=0) - onehot
    position = jnp.sum(before * onehot, axis=1)
    return (flat_ids * per_expert + position).astype(jnp.int32)


def spread_rows(pair_rows, slots, total_rows):
    empty = jnp.zeros((total_rows, pair_rows.shape[1]), pair_rows.dtype)
    return empty.at[slots].set(pair_rows)


def section_pass(items):
    arriving, returning, saved, ids_f, gates_f, ids_b, gates_b, w_gate, w_up, w_down = items
    per_expert = N_EXPERT * CAP
    total_rows = EXPERTS * per_expert
    weight_g = w_gate.reshape(EXPERTS, SPLIT, D, H_DEV).astype(jnp.float32)
    weight_u = w_up.reshape(EXPERTS, SPLIT, D, H_DEV).astype(jnp.float32)
    weight_d = w_down.reshape(EXPERTS, SPLIT, H_DEV, D).astype(jnp.float32)

    slots_f = slot_index(ids_f, EXPERTS, per_expert)
    pairs_f = jnp.broadcast_to(arriving[:, None, :], (TOKENS, TOP, D)).reshape(TOKENS * TOP, D)
    filled = spread_rows(pairs_f, slots_f, total_rows).reshape(EXPERTS, per_expert, D).astype(jnp.float32)
    gate_pre = jnp.einsum('erd,ejdh->ejrh', filled, weight_g)
    up_pre = jnp.einsum('erd,ejdh->ejrh', filled, weight_u)
    hidden = (jax.nn.silu(gate_pre) * up_pre).astype(jnp.bfloat16)
    partial_out = jnp.einsum('ejrh,ejhd->ejrd', hidden.astype(jnp.float32), weight_d).astype(jnp.bfloat16)
    summed = jnp.sum(partial_out.astype(jnp.float32), axis=1).reshape(total_rows, D)
    picked = summed[slots_f].reshape(TOKENS, TOP, D)
    forward_rows = jnp.sum(picked * gates_f[:, :, None], axis=1).astype(jnp.bfloat16)

    slots_b = slot_index(ids_b, EXPERTS, per_expert)
    pairs_x = jnp.broadcast_to(saved[:, None, :], (TOKENS, TOP, D)).reshape(TOKENS * TOP, D)
    pairs_g = (gates_b[:, :, None] * returning[:, None, :].astype(jnp.float32)).astype(jnp.bfloat16)
    pairs_g = pairs_g.reshape(TOKENS * TOP, D)
    saved_rows = spread_rows(pairs_x, slots_b, total_rows).reshape(EXPERTS, per_expert, D).astype(jnp.float32)
    grad_rows = spread_rows(pairs_g, slots_b, total_rows).reshape(EXPERTS, per_expert, D).astype(jnp.float32)
    gate_back = jnp.einsum('erd,ejdh->ejrh', saved_rows, weight_g)
    up_back = jnp.einsum('erd,ejdh->ejrh', saved_rows, weight_u)
    sigma = jax.nn.sigmoid(gate_back)
    hidden_grad = jnp.einsum('erd,ejhd->ejrh', grad_rows, weight_d)
    grad_gate = (hidden_grad * up_back * sigma * (1.0 + gate_back * (1.0 - sigma))).astype(jnp.bfloat16)
    grad_up = (hidden_grad * gate_back * sigma).astype(jnp.bfloat16)
    back_gate = jnp.einsum('ejrh,ejdh->ejrd', grad_gate.astype(jnp.float32), weight_g)
    back_up = jnp.einsum('ejrh,ejdh->ejrd', grad_up.astype(jnp.float32), weight_u)
    partial_in = (back_gate + back_up).astype(jnp.bfloat16)
    summed_in = jnp.sum(partial_in.astype(jnp.float32), axis=1).reshape(total_rows, D)
    picked_in = summed_in[slots_b].reshape(TOKENS, TOP, D)
    backward_rows = jnp.sum(picked_in, axis=1).astype(jnp.bfloat16)
    return forward_rows, backward_rows


def reference(handoff, grad_handoff, parked, ids_fwd, gates_fwd, ids_bwd, gates_bwd, w_gate, w_up, w_down):
    arriving = jnp.roll(handoff, 1, axis=0)
    returning = jnp.roll(grad_handoff, -1, axis=0)
    saved = jnp.roll(parked, SECTIONS // 2, axis=0)
    forward_out, backward_out = lax.map(section_pass, (arriving, returning, saved, ids_fwd, gates_fwd, ids_bwd, gates_bwd, w_gate, w_up, w_down))
    return forward_out, backward_out
```

```python
import jax
import jax.numpy as jnp
from jax import lax
from jax.experimental import pallas as pl
from jax.experimental.pallas import tpu as pltpu
from jax.sharding import PartitionSpec as P

EXPERTS = 8
CAP = 48
NY = 4
NZ = 4
TOK = 128
HALF = 64
D = 2560
HID = 384
ROWS = NY * CAP
NC = 512
STEPS = D // NC
F32 = jnp.float32
BF16 = jnp.bfloat16
NT = (((1,), (1,)), ((), ()))
N_COPIES = 93


def body(
    hand,
    grad,
    parked,
    meta,
    w_gate,
    w_up,
    w_down,
    out_f,
    out_b,
    wg,
    wu,
    wd,
    ids,
    pos_rows,
    gate_rows,
    pos_cols,
    gate_cols,
    x_s,
    x_r,
    x_f,
    in_s,
    in_r,
    in_f,
    stage,
    ret_b,
    ret_f,
    far,
    near,
    hop1,
    hop2,
    own_sum,
    acc_a,
    acc_u,
    acc_q,
    act_a,
    act_u,
    p_mat,
    q_mat,
    send_sem,
    recv_sem,
    local_sem,
):
    s = lax.axis_index("section")
    e = lax.axis_index("expert")
    y = e // NZ
    z = e % NZ
    zl = s // 8
    pair = z // 2

    def at(section, yy, zz):
        return (section, yy * NZ + zz)

    zp, zm, z2 = (z + 1) % 4, (z + 3) % 4, (z + 2) % 4
    nxt, prv, mate = (s + 1) % 16, (s + 15) % 16, (s + 8) % 16
    up_to = (z + zl) % 4
    down_to = (z + 3 + zl) % 4
    zp_dev, zm_dev, z2_dev = at(s, y, zp), at(s, y, zm), at(s, y, z2)
    y_dev = [None] + [at(s, (y + r) % 4, z) for r in (1, 2, 3)]

    counter = [0]
    pending = []

    def remote(src, dst, device):
        i = counter[0]
        counter[0] += 1
        copy = pltpu.make_async_remote_copy(
            src_ref=src,
            dst_ref=dst,
            send_sem=send_sem.at[i],
            recv_sem=recv_sem.at[i],
            device_id=device,
            device_id_type=pl.DeviceIdType.MESH,
        )
        pending.append(copy)
        return copy

    local = [
        pltpu.make_async_copy(w_gate.at[0, 0], wg, local_sem.at[0]),
        pltpu.make_async_copy(w_up.at[0, 0], wu, local_sem.at[1]),
        pltpu.make_async_copy(w_down.at[0, 0], wd, local_sem.at[2]),
    ]
    for copy in local:
        copy.start()
    ids[z] = meta[...]

    barrier = pltpu.get_barrier_semaphore()
    others = [at(nxt, y, z), at(prv, y, z), at(mate, y, up_to), at(mate, y, down_to)]
    others += [zp_dev, zm_dev, z2_dev] + y_dev[1:]
    for device in others:
        pl.semaphore_signal(barrier, inc=1, device_id=device, device_id_type=pl.DeviceIdType.MESH)
    pl.semaphore_wait(barrier, len(others))

    meta_copies = [remote(ids.at[z], ids.at[z], device) for device in (zp_dev, zm_dev, z2_dev)]
    for copy in meta_copies:
        copy.start()
    halves = (pl.ds(0, HALF), pl.ds(HALF, HALF))
    s_up = [remote(parked.at[0, h], x_s.at[z, h], at(mate, y, up_to)) for h in halves]
    s_down = [remote(parked.at[0, h], x_s.at[z, h], at(mate, y, down_to)) for h in halves]
    shift_r = remote(grad.at[0], x_r.at[z], at(prv, y, z))
    shift_f = remote(hand.at[0], x_f.at[z], at(nxt, y, z))
    shift_r.start()
    shift_f.start()
    for one, two in zip(s_up, s_down):
        one.start()
        two.start()

    for copy in meta_copies:
        copy.wait_recv()
    lower = lax.broadcasted_iota(jnp.int32, (TOK, TOK), 0) < lax.broadcasted_iota(
        jnp.int32, (TOK, TOK), 1
    )
    lower = lower.astype(F32).astype(BF16)
    expert_row = lax.broadcasted_iota(jnp.int32, (EXPERTS, TOK), 0).astype(F32)
    filler = jnp.zeros((TOK - EXPERTS, TOK), F32)
    for zz in range(NZ):
        for which in range(2):
            base = 4 * which
            first = ids[zz, base : base + 1, :] == expert_row
            second = ids[zz, base + 1 : base + 2, :] == expert_row
            named = jnp.where(first | second, 1.0, 0.0)
            before = jnp.dot(named.astype(BF16), lower, preferred_element_type=F32)
            place = jnp.where(named > 0.5, before, -1.0)
            gate = jnp.where(first, ids[zz, base + 2 : base + 3, :], 0.0) + jnp.where(
                second, ids[zz, base + 3 : base + 4, :], 0.0
            )
            pos_rows[which, zz] = place
            gate_rows[which, zz] = gate
            pos_cols[which, zz] = jnp.concatenate([place, filler], axis=0).T
            gate_cols[which, zz] = jnp.concatenate([gate, filler], axis=0).T

    experts = [((y + r) % 4) * 2 + pair for r in range(NY)]
    slot_row = lax.broadcasted_iota(jnp.int32, (CAP, TOK), 0).astype(F32)
    own_rows = pl.ds(pl.multiple_of(y * CAP, 16), CAP)

    def columns(i):
        return pl.ds(pl.multiple_of(i * NC, NC), NC)

    def pack(which, zz, source, target, slot, scaled):
        picks = []
        gates = []
        for r in range(NY):
            one = jnp.where(slot_row == pos_rows[which, zz, pl.ds(experts[r], 1), :], 1.0, 0.0)
            picks.append(one)
            if scaled:
                gates.append(
                    jnp.sum(one * gate_rows[which, zz, pl.ds(experts[r], 1), :], axis=1, keepdims=True)
                )
        p_mat[...] = jnp.concatenate(picks, axis=0).astype(BF16)
        gate = jnp.concatenate(gates, axis=0) if scaled else None

        @pl.loop(0, STEPS)
        def _(i):
            c = columns(i)
            rows = jnp.dot(p_mat[...], source[zz, :, c], preferred_element_type=F32)
            if scaled:
                rows = rows * gate
            rows = rows.astype(BF16)
            target[zz, own_rows, c] = rows[:CAP]
            stage[slot, :, c] = rows[CAP:]

        copies = []
        for r in (1, 2, 3):
            copy = remote(
                stage.at[slot, pl.ds((r - 1) * CAP, CAP)], target.at[zz, own_rows], y_dev[r]
            )
            copy.start()
            copies.append(copy)
        return copies

    def forward(zz):
        acc_a[...] = jnp.zeros_like(acc_a)
        acc_u[...] = jnp.zeros_like(acc_u)

        @pl.loop(0, STEPS)
        def _(i):
            c = columns(i)
            rows = in_f[zz, :, c]
            acc_a[...] += jnp.dot(rows, wg[c, :], preferred_element_type=F32)
            acc_u[...] += jnp.dot(rows, wu[c, :], preferred_element_type=F32)

        a = acc_a[...]
        act_a[...] = (a / (1.0 + jnp.exp(-a)) * acc_u[...]).astype(BF16)

        @pl.loop(0, STEPS)
        def _(i):
            c = columns(i)
            in_f[zz, :, c] = jnp.dot(act_a[...], wd[:, c], preferred_element_type=F32).astype(BF16)

    def backward(zz):
        acc_a[...] = jnp.zeros_like(acc_a)
        acc_u[...] = jnp.zeros_like(acc_u)
        acc_q[...] = jnp.zeros_like(acc_q)

        @pl.loop(0, STEPS)
        def _(i):
            c = columns(i)
            rows = in_s[zz, :, c]
            acc_a[...] += jnp.dot(rows, wg[c, :], preferred_element_type=F32)
            acc_u[...] += jnp.dot(rows, wu[c, :], preferred_element_type=F32)
            acc_q[...] += lax.dot_general(in_r[zz, :, c], wd[:, c], NT, preferred_element_type=F32)

        a = acc_a[...]
        q = acc_q[...]
        sigma = 1.0 / (1.0 + jnp.exp(-a))
        act_a[...] = (q * acc_u[...] * sigma * (1.0 + a * (1.0 - sigma))).astype(BF16)
        act_u[...] = (q * a * sigma).astype(BF16)

        @pl.loop(0, STEPS)
        def _(i):
            c = columns(i)
            back = lax.dot_general(act_a[...], wg[c, :], NT, preferred_element_type=F32)
            back += lax.dot_general(act_u[...], wu[c, :], NT, preferred_element_type=F32)
            in_r[zz, :, c] = back.astype(BF16)

    def send_back(zz, result, returned):
        copies = []
        for r in (1, 2, 3):
            rows = pl.ds(pl.multiple_of(((y + r) % 4) * CAP, 16), CAP)
            copy = remote(
                result.at[zz, rows], returned.at[zz, pl.ds((4 - r) * CAP, CAP)], y_dev[r]
            )
            copy.start()
            copies.append(copy)
        returned[zz, pl.ds(0, CAP), :] = result[zz, own_rows, :]
        return copies

    lane = lax.broadcasted_iota(jnp.int32, (TOK, ROWS), 1)
    block = jnp.where(lane >= CAP, 1, 0) + jnp.where(lane >= 2 * CAP, 1, 0)
    block = block + jnp.where(lane >= 3 * CAP, 1, 0)
    slot_col = (lane - block * CAP).astype(F32)
    expert_lane = lax.broadcasted_iota(jnp.int32, (TOK, TOK), 1)

    def spread(table, which, zz):
        cols = table[which, zz]
        wide = jnp.zeros((TOK, ROWS), F32)
        for r in range(NY):
            one = jnp.sum(jnp.where(expert_lane == experts[r], cols, 0.0), axis=1, keepdims=True)
            wide = wide + jnp.where(block == r, one, 0.0)
        return wide

    def combine(which, zz, returned, store):
        weight = jnp.where(spread(pos_cols, which, zz) == slot_col, 1.0, 0.0)
        if which == 0:
            weight = weight * spread(gate_cols, which, zz)
            high = weight.astype(BF16)
            p_low = (weight - high.astype(F32)).astype(BF16)
            q_mat[0] = high
            q_mat[1] = p_low
        else:
            q_mat[0] = weight.astype(BF16)

        @pl.loop(0, STEPS)
        def _(i):
            c = columns(i)
            total = jnp.dot(q_mat[0], returned[zz, :, c], preferred_element_type=F32)
            if which == 0:
                total += jnp.dot(q_mat[1], returned[zz, :, c], preferred_element_type=F32)
            store(c, total)

    def landed(copies):
        for copy in copies:
            copy.wait_recv()

    def to_far(which, returned):
        def store(c, total):
            far[which, :, c] = total.astype(BF16)

        combine(which, z2, returned, store)
        up = remote(far.at[which, halves[0]], hop1.at[which, 0], zp_dev)
        down = remote(far.at[which, halves[1]], hop1.at[which, 1], zm_dev)
        up.start()
        down.start()
        return up, down

    def to_near(which, returned, direction, arriving):
        zz = zp if direction == 0 else zm
        device = zp_dev if direction == 0 else zm_dev
        through, free = halves[direction], halves[1 - direction]

        def store(c, total):
            near[which, direction, :, c] = total.astype(BF16)

        combine(which, zz, returned, store)
        first = remote(near.at[which, direction, free], hop2.at[which, direction, free], device)
        first.start()
        arriving.wait_recv()
        near[which, direction, through, :] = (
            near[which, direction, through, :].astype(F32) + hop1[which, direction].astype(F32)
        ).astype(BF16)
        second = remote(
            near.at[which, direction, through], hop2.at[which, direction, through], device
        )
        second.start()
        return [first, second]

    def to_own(which, returned):
        def store(c, total):
            own_sum[which, :, c] = total

        combine(which, z, returned, store)

    def finish(which, out):
        out[0] = (
            own_sum[which] + hop2[which, 0].astype(F32) + hop2[which, 1].astype(F32)
        ).astype(BF16)

    def spread_first(x):
        return [
            remote(x.at[z], x.at[z], zp_dev),
            remote(x.at[z], x.at[z], zm_dev),
        ]

    def spread_second(x):
        return [
            remote(x.at[zm, halves[0]], x.at[zm, halves[0]], zp_dev),
            remote(x.at[zp, halves[1]], x.at[zp, halves[1]], zm_dev),
        ]

    def start(copies):
        for copy in copies:
            copy.start()

    zs_up, zs_down = (z + 3 + zl) % 4, (z + zl) % 4
    zs_up2, zs_down2 = (z + 2 + zl) % 4, (z + 1 + zl) % 4

    shift_r.wait_recv()
    got_r_own = pack(1, z, x_r, in_r, 0, True)
    shift_f.wait_recv()
    got_f_own = pack(0, z, x_f, in_f, 1, False)

    s_up2 = [remote(x_s.at[zs_up, h], x_s.at[zs_up, h], zp_dev) for h in halves]
    s_down2 = [remote(x_s.at[zs_down, h], x_s.at[zs_down, h], zm_dev) for h in halves]
    for i in range(2):
        s_up[i].wait_recv()
        s_up2[i].start()
        s_down[i].wait_recv()
        s_down2[i].start()

    got_s = [pack(1, zs_up, x_s, in_s, 2, False), pack(1, zs_down, x_s, in_s, 3, False)]
    r_first = spread_first(x_r)
    start(r_first)

    for copy in local:
        copy.wait()
    landed(got_f_own)
    forward(z)

    landed(s_up2)
    got_s.append(pack(1, zs_up2, x_s, in_s, 4, False))
    landed(s_down2)
    got_s.append(pack(1, zs_down2, x_s, in_s, 5, False))

    landed(r_first)
    r_second = spread_second(x_r)
    start(r_second)
    f_first = spread_first(x_f)
    start(f_first)
    got_r_m = pack(1, zm, x_r, in_r, 6, True)
    got_r_p = pack(1, zp, x_r, in_r, 7, True)

    landed(got_r_own)
    for copies in got_s:
        landed(copies)
    backward(z)

    landed(r_second)
    got_r_2 = pack(1, z2, x_r, in_r, 8, True)
    back_own = send_back(z, in_r, ret_b)
    landed(got_r_m)
    backward(zm)
    landed(got_r_p)
    backward(zp)
    landed(f_first)
    f_second = spread_second(x_f)
    start(f_second)
    landed(got_r_2)
    backward(z2)
    back_2 = send_back(z2, in_r, ret_b)
    back_p = send_back(zp, in_r, ret_b)
    back_m = send_back(zm, in_r, ret_b)
    got_f_m = pack(0, zm, x_f, in_f, 9, False)
    got_f_p = pack(0, zp, x_f, in_f, 10, False)
    landed(f_second)
    got_f_2 = pack(0, z2, x_f, in_f, 11, False)
    landed(back_2)
    b_up, b_down = to_far(1, ret_b)
    landed(back_p)
    b_near = to_near(1, ret_b, 0, b_up)
    landed(back_m)
    b_near += to_near(1, ret_b, 1, b_down)
    landed(back_own)
    to_own(1, ret_b)

    landed(got_f_m)
    forward(zm)
    landed(got_f_p)
    forward(zp)
    landed(got_f_2)
    forward(z2)
    fore_2 = send_back(z2, in_f, ret_f)
    fore_p = send_back(zp, in_f, ret_f)
    fore_m = send_back(zm, in_f, ret_f)
    fore_own = send_back(z, in_f, ret_f)
    landed(b_near)
    finish(1, out_b)
    landed(fore_2)
    f_up, f_down = to_far(0, ret_f)
    landed(fore_p)
    f_near = to_near(0, ret_f, 0, f_up)
    landed(fore_m)
    f_near += to_near(0, ret_f, 1, f_down)
    landed(fore_own)
    to_own(0, ret_f)
    landed(f_near)
    finish(0, out_f)

    for copy in pending:
        copy.wait_send()
    assert counter[0] == N_COPIES, counter[0]


def on_device(
    handoff, grad_handoff, parked, ids_fwd, gates_fwd, ids_bwd, gates_bwd, w_gate, w_up, w_down
):
    meta = jnp.concatenate(
        [ids_fwd[0].astype(F32), gates_fwd[0], ids_bwd[0].astype(F32), gates_bwd[0]], axis=1
    ).T
    anywhere = pl.BlockSpec(memory_space=pl.ANY)
    vmem = pl.BlockSpec(memory_space=pltpu.VMEM)
    result = jax.ShapeDtypeStruct((1, TOK, D), BF16)
    return pl.pallas_call(
        body,
        out_shape=(result, result),
        in_specs=[anywhere] * 3 + [vmem] + [anywhere] * 3,
        out_specs=(vmem, vmem),
        scratch_shapes=[
            pltpu.VMEM((D, HID), BF16),
            pltpu.VMEM((D, HID), BF16),
            pltpu.VMEM((HID, D), BF16),
            pltpu.VMEM((NZ, 8, TOK), F32),
            pltpu.VMEM((2, NZ, EXPERTS, TOK), F32),
            pltpu.VMEM((2, NZ, EXPERTS, TOK), F32),
            pltpu.VMEM((2, NZ, TOK, TOK), F32),
            pltpu.VMEM((2, NZ, TOK, TOK), F32),
            pltpu.VMEM((NZ, TOK, D), BF16),
            pltpu.VMEM((NZ, TOK, D), BF16),
            pltpu.VMEM((NZ, TOK, D), BF16),
            pltpu.VMEM((NZ, ROWS, D), BF16),
            pltpu.VMEM((NZ, ROWS, D), BF16),
            pltpu.VMEM((NZ, ROWS, D), BF16),
            pltpu.VMEM((12, ROWS - CAP, D), BF16),
            pltpu.VMEM((NZ, ROWS, D), BF16),
            pltpu.VMEM((NZ, ROWS, D), BF16),
            pltpu.VMEM((2, TOK, D), BF16),
            pltpu.VMEM((2, 2, TOK, D), BF16),
            pltpu.VMEM((2, 2, HALF, D), BF16),
            pltpu.VMEM((2, 2, TOK, D), BF16),
            pltpu.VMEM((2, TOK, D), F32),
            pltpu.VMEM((ROWS, HID), F32),
            pltpu.VMEM((ROWS, HID), F32),
            pltpu.VMEM((ROWS, HID), F32),
            pltpu.VMEM((ROWS, HID), BF16),
            pltpu.VMEM((ROWS, HID), BF16),
            pltpu.VMEM((ROWS, TOK), BF16),
            pltpu.VMEM((2, TOK, ROWS), BF16),
            pltpu.SemaphoreType.DMA((N_COPIES,)),
            pltpu.SemaphoreType.DMA((N_COPIES,)),
            pltpu.SemaphoreType.DMA((3,)),
        ],
        compiler_params=pltpu.CompilerParams(
            collective_id=0, has_side_effects=True, vmem_limit_bytes=62 * 2**20
        ),
        name="relay_experts",
    )(handoff, grad_handoff, parked, meta, w_gate, w_up, w_down)


def solution(mesh):
    rows = P("section", "expert", None)
    weights = P("section", "expert", None, None)
    return jax.shard_map(
        on_device,
        mesh=mesh,
        in_specs=(rows,) * 7 + (weights,) * 3,
        out_specs=(rows, rows),
        check_vma=False,
    )
```

```python
import jax
import jax.numpy as jnp
from jax import lax
from jax.experimental import pallas as pl
from jax.experimental.pallas import tpu as pltpu
from jax.sharding import PartitionSpec as P

EXPERTS = 8
CAP = 48
NY = 4
NZ = 4
TOK = 128
HALF = 64
D = 2560
HID = 384
ROWS = NY * CAP
NC = 512
PACK = 640
STEPS = D // NC
F32 = jnp.float32
BF16 = jnp.bfloat16
NT = (((1,), (1,)), ((), ()))
N_COPIES = 115


def body(
    hand,
    grad,
    parked,
    meta,
    w_gate,
    w_up,
    w_down,
    out,
    wg,
    wu,
    wd,
    ids,
    pos_rows,
    gate_rows,
    pos_cols,
    gate_cols,
    x_s,
    x_r,
    x_f,
    in_s,
    in_r,
    in_f,
    stage,
    ret_b,
    ret_f,
    far,
    near,
    hop1,
    hop2,
    own_sum,
    acc_a,
    acc_u,
    acc_q,
    act_a,
    act_u,
    p_mat,
    q_mat,
    send_sem,
    recv_sem,
    local_sem,
):
    s = lax.axis_index("section")
    e = lax.axis_index("expert")
    y = e // NZ
    z = e % NZ
    zl = s // 8
    pair = z // 2

    def at(section, yy, zz):
        return (section, yy * NZ + zz)

    zp, zm, z2 = (z + 1) % 4, (z + 3) % 4, (z + 2) % 4
    nxt, prv, mate = (s + 1) % 16, (s + 15) % 16, (s + 8) % 16
    up_to = (z + zl) % 4
    down_to = (z + 3 + zl) % 4
    zp_dev, zm_dev, z2_dev = at(s, y, zp), at(s, y, zm), at(s, y, z2)
    y_dev = [None] + [at(s, (y + r) % 4, z) for r in (1, 2, 3)]

    counter = [0]
    pending = []

    def remote(src, dst, device):
        i = counter[0]
        counter[0] += 1
        copy = pltpu.make_async_remote_copy(
            src_ref=src,
            dst_ref=dst,
            send_sem=send_sem.at[i],
            recv_sem=recv_sem.at[i],
            device_id=device,
            device_id_type=pl.DeviceIdType.MESH,
        )
        pending.append(copy)
        return copy

    local = [
        pltpu.make_async_copy(w_gate.at[0, 0], wg, local_sem.at[0]),
        pltpu.make_async_copy(w_up.at[0, 0], wu, local_sem.at[1]),
        pltpu.make_async_copy(w_down.at[0, 0], wd, local_sem.at[2]),
    ]
    for copy in local:
        copy.start()
    ids[z] = meta[...]

    lower = lax.broadcasted_iota(jnp.int32, (TOK, TOK), 0) < lax.broadcasted_iota(
        jnp.int32, (TOK, TOK), 1
    )
    lower = lower.astype(F32).astype(BF16)
    expert_row = lax.broadcasted_iota(jnp.int32, (EXPERTS, TOK), 0).astype(F32)
    filler = jnp.zeros((TOK - EXPERTS, TOK), F32)

    def tables(zz):
        for which in range(2):
            base = 4 * which
            one = ids[zz, base : base + 1, :]
            two = ids[zz, base + 1 : base + 2, :]
            first = one == expert_row
            second = two == expert_row
            named = jnp.where(first | second, 1.0, 0.0)
            before = jnp.dot(named.astype(BF16), lower, preferred_element_type=F32)
            place = jnp.where(named > 0.5, before, -1.0)
            gate = jnp.where(first, ids[zz, base + 2 : base + 3, :], 0.0) + jnp.where(
                second, ids[zz, base + 3 : base + 4, :], 0.0
            )
            pos_rows[which, zz] = place
            gate_rows[which, zz] = gate
            pos_cols[which, zz] = jnp.concatenate([place, filler], axis=0).T
            gate_cols[which, zz] = jnp.concatenate([gate, filler], axis=0).T

    barrier = pltpu.get_barrier_semaphore()
    others = [at(nxt, y, z), at(prv, y, z), at(mate, y, up_to), at(mate, y, down_to)]
    others += [zp_dev, zm_dev, z2_dev] + y_dev[1:]
    for device in others:
        pl.semaphore_signal(barrier, inc=1, device_id=device, device_id_type=pl.DeviceIdType.MESH)
    tables(z)
    pl.semaphore_wait(barrier, len(others))

    meta_copies = [remote(ids.at[z], ids.at[z], device) for device in (zp_dev, zm_dev, z2_dev)]
    for copy in meta_copies:
        copy.start()
    halves = (pl.ds(0, HALF), pl.ds(HALF, HALF))
    s_up = [remote(parked.at[0, h], x_s.at[z, h], at(mate, y, up_to)) for h in halves]
    s_down = [remote(parked.at[0, h], x_s.at[z, h], at(mate, y, down_to)) for h in halves]
    wide = (pl.ds(0, D // 2), pl.ds(D // 2, D // 2))
    shift = [
        [remote(hand.at[0, :, c], x_f.at[z, :, c], at(nxt, y, z)) for c in wide],
        [remote(grad.at[0, :, c], x_r.at[z, :, c], at(prv, y, z)) for c in wide],
    ]
    for i in range(2):
        shift[1][i].start()
        shift[0][i].start()
    for one, two in zip(s_up, s_down):
        one.start()
        two.start()

    experts = [((y + r) % 4) * 2 + pair for r in range(NY)]
    slot_row = lax.broadcasted_iota(jnp.int32, (CAP, TOK), 0).astype(F32)
    own_rows = pl.ds(pl.multiple_of(y * CAP, 16), CAP)

    def columns(i):
        return pl.ds(pl.multiple_of(i * NC, NC), NC)

    def sort_rows(which, zz, source, target, slot, scaled):
        picks = []
        gates = []
        for r in range(NY):
            one = jnp.where(slot_row == pos_rows[which, zz, pl.ds(experts[r], 1), :], 1.0, 0.0)
            picks.append(one)
            if scaled:
                gates.append(
                    jnp.sum(one * gate_rows[which, zz, pl.ds(experts[r], 1), :], axis=1, keepdims=True)
                )
        p_mat[...] = jnp.concatenate(picks, axis=0).astype(BF16)
        gate = jnp.concatenate(gates, axis=0) if scaled else None

        def some(first, last):
            @pl.loop(first, last)
            def _(i):
                c = pl.ds(pl.multiple_of(i * PACK, PACK), PACK)
                rows = jnp.dot(p_mat[...], source[zz, :, c], preferred_element_type=F32)
                if scaled:
                    rows = rows * gate
                rows = rows.astype(BF16)
                target[zz, own_rows, c] = rows[:CAP]
                stage[slot, :, c] = rows[CAP:]

        return some

    def along_y(zz, target, slot, c):
        return [
            remote(
                stage.at[slot, pl.ds((r - 1) * CAP, CAP), c],
                target.at[zz, own_rows, c],
                y_dev[r],
            )
            for r in (1, 2, 3)
        ]

    def pack(which, zz, source, target, slot, scaled):
        sort_rows(which, zz, source, target, slot, scaled)(0, D // PACK)
        copies = along_y(zz, target, slot, pl.ds(0, D))
        for copy in copies:
            copy.start()
        return copies

    def forward(zz):
        acc_a[...] = jnp.zeros_like(acc_a)
        acc_u[...] = jnp.zeros_like(acc_u)

        @pl.loop(0, STEPS)
        def _(i):
            c = columns(i)
            rows = in_f[zz, :, c]
            acc_a[...] += jnp.dot(rows, wg[c, :], preferred_element_type=F32)
            acc_u[...] += jnp.dot(rows, wu[c, :], preferred_element_type=F32)

        a = acc_a[...]
        act_a[...] = (a / (1.0 + jnp.exp(-a)) * acc_u[...]).astype(BF16)

        @pl.loop(0, STEPS)
        def _(i):
            c = columns(i)
            in_f[zz, :, c] = jnp.dot(act_a[...], wd[:, c], preferred_element_type=F32).astype(BF16)

    def backward(zz):
        acc_a[...] = jnp.zeros_like(acc_a)
        acc_u[...] = jnp.zeros_like(acc_u)
        acc_q[...] = jnp.zeros_like(acc_q)

        @pl.loop(0, STEPS)
        def _(i):
            c = columns(i)
            rows = in_s[zz, :, c]
            acc_a[...] += jnp.dot(rows, wg[c, :], preferred_element_type=F32)
            acc_u[...] += jnp.dot(rows, wu[c, :], preferred_element_type=F32)
            acc_q[...] += lax.dot_general(in_r[zz, :, c], wd[:, c], NT, preferred_element_type=F32)

        a = acc_a[...]
        q = acc_q[...]
        sigma = 1.0 / (1.0 + jnp.exp(-a))
        act_a[...] = (q * acc_u[...] * sigma * (1.0 + a * (1.0 - sigma))).astype(BF16)
        act_u[...] = (q * a * sigma).astype(BF16)

        @pl.loop(0, STEPS)
        def _(i):
            c = columns(i)
            back = lax.dot_general(act_a[...], wg[c, :], NT, preferred_element_type=F32)
            back += lax.dot_general(act_u[...], wu[c, :], NT, preferred_element_type=F32)
            in_r[zz, :, c] = back.astype(BF16)

    def send_back(zz, result, returned, c=pl.ds(0, D)):
        copies = []
        for r in (1, 2, 3):
            rows = pl.ds(pl.multiple_of(((y + r) % 4) * CAP, 16), CAP)
            copy = remote(
                result.at[zz, rows, c], returned.at[zz, pl.ds((4 - r) * CAP, CAP), c], y_dev[r]
            )
            copy.start()
            copies.append(copy)
        returned[zz, pl.ds(0, CAP), c] = result[zz, own_rows, c]
        return copies

    lane = lax.broadcasted_iota(jnp.int32, (TOK, ROWS), 1)
    block = jnp.where(lane >= CAP, 1, 0) + jnp.where(lane >= 2 * CAP, 1, 0)
    block = block + jnp.where(lane >= 3 * CAP, 1, 0)
    slot_col = (lane - block * CAP).astype(F32)
    expert_lane = lax.broadcasted_iota(jnp.int32, (TOK, TOK), 1)

    def spread(table, which, zz):
        cols = table[which, zz]
        wide = jnp.zeros((TOK, ROWS), F32)
        for r in range(NY):
            one = jnp.sum(jnp.where(expert_lane == experts[r], cols, 0.0), axis=1, keepdims=True)
            wide = wide + jnp.where(block == r, one, 0.0)
        return wide

    def combine(which, zz, returned, store, first=0, last=D // PACK):
        weight = jnp.where(spread(pos_cols, which, zz) == slot_col, 1.0, 0.0)
        if which == 0:
            weight = weight * spread(gate_cols, which, zz)
            high = weight.astype(BF16)
            p_low = (weight - high.astype(F32)).astype(BF16)
            q_mat[0] = high
            q_mat[1] = p_low
        else:
            q_mat[0] = weight.astype(BF16)

        @pl.loop(first, last)
        def _(i):
            c = pl.ds(pl.multiple_of(i * PACK, PACK), PACK)
            total = jnp.dot(q_mat[0], returned[zz, :, c], preferred_element_type=F32)
            if which == 0:
                total += jnp.dot(q_mat[1], returned[zz, :, c], preferred_element_type=F32)
            store(c, total)

    def landed(copies):
        for copy in copies:
            copy.wait_recv()

    def to_far(which, returned):
        def store(c, total):
            far[which, :, c] = total.astype(BF16)

        combine(which, z2, returned, store)
        up = remote(far.at[which, halves[0]], hop1.at[which, 0], zp_dev)
        down = remote(far.at[which, halves[1]], hop1.at[which, 1], zm_dev)
        up.start()
        down.start()
        return up, down

    def to_near(which, returned, direction, arriving, parts):
        zz = zp if direction == 0 else zm
        device = zp_dev if direction == 0 else zm_dev
        through, free = halves[direction], halves[1 - direction]

        def store(c, total):
            near[which, direction, :, c] = total.astype(BF16)

        copies = []
        for i, part in enumerate(parts):
            landed(part)
            steps = D // PACK // len(parts)
            c = pl.ds(i * steps * PACK, steps * PACK)
            combine(which, zz, returned, store, i * steps, (i + 1) * steps)
            first = remote(
                near.at[which, direction, free, c], hop2.at[which, direction, free, c], device
            )
            first.start()
            if i == 0:
                arriving.wait_recv()
            near[which, direction, through, c] = (
                near[which, direction, through, c].astype(F32)
                + hop1[which, direction, :, c].astype(F32)
            ).astype(BF16)
            second = remote(
                near.at[which, direction, through, c], hop2.at[which, direction, through, c], device
            )
            second.start()
            copies += [first, second]
        return copies

    def to_own(which, returned):
        def store(c, total):
            own_sum[which, :, c] = total

        combine(which, z, returned, store)

    def finish(which, out):
        out[which] = (
            own_sum[which] + hop2[which, 0].astype(F32) + hop2[which, 1].astype(F32)
        ).astype(BF16)

    def spread_first(x, through):
        one, two = (halves[0], halves[1]) if through else (halves[1], halves[0])
        return [
            remote(x.at[z, one], x.at[z, one], zp_dev),
            remote(x.at[z, two], x.at[z, two], zm_dev),
        ]

    def spread_second(x):
        return [
            remote(x.at[zm, halves[0]], x.at[zm, halves[0]], zp_dev),
            remote(x.at[zp, halves[1]], x.at[zp, halves[1]], zm_dev),
        ]

    def nearby(copies):
        copies[0].wait_recv()
        copies[2].wait_recv()

    def straight(copies):
        copies[1].wait_recv()

    def start(copies):
        for copy in copies:
            copy.start()

    zs_up, zs_down = (z + 3 + zl) % 4, (z + zl) % 4
    zs_up2, zs_down2 = (z + 2 + zl) % 4, (z + 1 + zl) % 4

    own = [
        [along_y(z, in_f, 0, c) for c in wide],
        [along_y(z, in_r, 1, c) for c in wide],
    ]
    got_f_own, got_r_own = own[0][0] + own[0][1], own[1][0] + own[1][1]

    def own_rows_out(which):
        some = sort_rows(which, z, (x_f, x_r)[which], (in_f, in_r)[which], which, which == 1)
        for i in range(2):
            shift[which][i].wait_recv()
            some(i * D // PACK // 2, (i + 1) * D // PACK // 2)
            start(own[which][i])

    s_up2 = [remote(x_s.at[zs_up, h], x_s.at[zs_up, h], zp_dev) for h in halves]
    s_down2 = [remote(x_s.at[zs_down, h], x_s.at[zs_down, h], zm_dev) for h in halves]

    odd = s % 2 == 1

    @pl.when(odd)
    def _():
        own_rows_out(0)

    @pl.when(jnp.logical_not(odd))
    def _():
        own_rows_out(1)

    for copy in meta_copies:
        copy.wait_recv()
    for zz in (zp, zm, z2):
        tables(zz)

    for i in range(2):
        s_up[i].wait_recv()
        s_up2[i].start()
        s_down[i].wait_recv()
        s_down2[i].start()

    @pl.when(odd)
    def _():
        own_rows_out(1)

    @pl.when(jnp.logical_not(odd))
    def _():
        own_rows_out(0)

    got_s = [pack(1, zs_up, x_s, in_s, 2, False), pack(1, zs_down, x_s, in_s, 3, False)]
    for copy in local:
        copy.wait()

    r_first_a, r_first_b = spread_first(x_r, True), spread_first(x_r, False)
    f_first_a, f_first_b = spread_first(x_f, True), spread_first(x_f, False)
    r_second, f_second = spread_second(x_r), spread_second(x_f)

    landed([s_up2[0], s_down2[0]])
    start(r_first_a)
    landed(got_f_own)
    forward(z)
    landed([s_up2[1], s_down2[1]])
    start(r_first_b)
    got_s.append(pack(1, zs_up2, x_s, in_s, 4, False))
    got_s.append(pack(1, zs_down2, x_s, in_s, 5, False))
    fore_own = send_back(z, in_f, ret_f)

    landed(r_first_a)
    start(r_second)
    landed(r_first_b)
    start(f_first_a)
    got_r_p = pack(1, zp, x_r, in_r, 6, True)
    got_r_m = pack(1, zm, x_r, in_r, 7, True)
    landed(got_r_own)
    for copies in got_s:
        landed(copies)
    backward(z)
    landed(r_second)
    start(f_first_b)
    got_r_2 = pack(1, z2, x_r, in_r, 8, True)
    landed(got_r_p)
    backward(zp)
    back_p = send_back(zp, in_r, ret_b)
    landed(f_first_a)
    start(f_second)
    landed(got_r_2)
    backward(z2)
    back_2 = send_back(z2, in_r, ret_b)
    landed(got_r_m)
    backward(zm)
    landed(f_first_b)
    nearby(back_2)
    back_m = send_back(zm, in_r, ret_b)
    straight(back_2)
    b_up, b_down = to_far(1, ret_b)
    landed(f_second)
    got_f_2 = pack(0, z2, x_f, in_f, 9, False)
    b_near = to_near(1, ret_b, 0, b_up, [back_p])
    got_f_p = pack(0, zp, x_f, in_f, 10, False)
    b_near += to_near(1, ret_b, 1, b_down, [back_m])
    landed(got_f_2)
    forward(z2)
    fore_2 = send_back(z2, in_f, ret_f)
    got_f_m = pack(0, zm, x_f, in_f, 11, False)
    landed(got_f_p)
    forward(zp)
    nearby(fore_2)
    fore_p = [send_back(zp, in_f, ret_f, c) for c in wide]
    straight(fore_2)
    f_up, f_down = to_far(0, ret_f)
    landed(got_f_m)
    forward(zm)
    fore_m = [send_back(zm, in_f, ret_f, c) for c in wide]
    landed(fore_own)
    to_own(0, ret_f)
    f_near = to_near(0, ret_f, 0, f_up, fore_p)
    back_own = send_back(z, in_r, ret_b)
    f_near += to_near(0, ret_f, 1, f_down, fore_m)
    landed(back_own)
    to_own(1, ret_b)
    landed(b_near)
    finish(1, out)
    landed(f_near)
    finish(0, out)

    for copy in pending:
        copy.wait_send()
    assert counter[0] == N_COPIES, counter[0]


def part_ways(both, out_f, out_b):
    out_f[0] = both[0]
    out_b[0] = both[1]


def on_device(
    handoff, grad_handoff, parked, ids_fwd, gates_fwd, ids_bwd, gates_bwd, w_gate, w_up, w_down
):
    meta = jnp.concatenate(
        [ids_fwd[0].astype(F32), gates_fwd[0], ids_bwd[0].astype(F32), gates_bwd[0]], axis=1
    ).T
    anywhere = pl.BlockSpec(memory_space=pl.ANY)
    vmem = pl.BlockSpec(memory_space=pltpu.VMEM)
    both = pl.pallas_call(
        body,
        out_shape=jax.ShapeDtypeStruct((2, TOK, D), BF16),
        in_specs=[anywhere] * 3 + [vmem] + [anywhere] * 3,
        out_specs=vmem,
        scratch_shapes=[
            pltpu.VMEM((D, HID), BF16),
            pltpu.VMEM((D, HID), BF16),
            pltpu.VMEM((HID, D), BF16),
            pltpu.VMEM((NZ, 8, TOK), F32),
            pltpu.VMEM((2, NZ, EXPERTS, TOK), F32),
            pltpu.VMEM((2, NZ, EXPERTS, TOK), F32),
            pltpu.VMEM((2, NZ, TOK, TOK), F32),
            pltpu.VMEM((2, NZ, TOK, TOK), F32),
            pltpu.VMEM((NZ, TOK, D), BF16),
            pltpu.VMEM((NZ, TOK, D), BF16),
            pltpu.VMEM((NZ, TOK, D), BF16),
            pltpu.VMEM((NZ, ROWS, D), BF16),
            pltpu.VMEM((NZ, ROWS, D), BF16),
            pltpu.VMEM((NZ, ROWS, D), BF16),
            pltpu.VMEM((12, ROWS - CAP, D), BF16),
            pltpu.VMEM((NZ, ROWS, D), BF16),
            pltpu.VMEM((NZ, ROWS, D), BF16),
            pltpu.VMEM((2, TOK, D), BF16),
            pltpu.VMEM((2, 2, TOK, D), BF16),
            pltpu.VMEM((2, 2, HALF, D), BF16),
            pltpu.VMEM((2, 2, TOK, D), BF16),
            pltpu.VMEM((2, TOK, D), F32),
            pltpu.VMEM((ROWS, HID), F32),
            pltpu.VMEM((ROWS, HID), F32),
            pltpu.VMEM((ROWS, HID), F32),
            pltpu.VMEM((ROWS, HID), BF16),
            pltpu.VMEM((ROWS, HID), BF16),
            pltpu.VMEM((ROWS, TOK), BF16),
            pltpu.VMEM((2, TOK, ROWS), BF16),
            pltpu.SemaphoreType.DMA((N_COPIES,)),
            pltpu.SemaphoreType.DMA((N_COPIES,)),
            pltpu.SemaphoreType.DMA((3,)),
        ],
        compiler_params=pltpu.CompilerParams(
            collective_id=0, has_side_effects=True, vmem_limit_bytes=62 * 2**20
        ),
        name="relay_experts",
    )(handoff, grad_handoff, parked, meta, w_gate, w_up, w_down)

    result = jax.ShapeDtypeStruct((1, TOK, D), BF16)
    return pl.pallas_call(
        part_ways,
        out_shape=(result, result),
        in_specs=[vmem],
        out_specs=(vmem, vmem),
        name="part_ways",
    )(both)


def solution(mesh):
    rows = P("section", "expert", None)
    weights = P("section", "expert", None, None)
    return jax.shard_map(
        on_device,
        mesh=mesh,
        in_specs=(rows,) * 7 + (weights,) * 3,
        out_specs=(rows, rows),
        check_vma=False,
    )
```

```python
import jax
import jax.numpy as jnp
from jax import lax
from jax.experimental import pallas as pl
from jax.experimental.pallas import tpu as pltpu
from jax.sharding import PartitionSpec as P

EXPERTS = 8
CAP = 48
NY = 4
NZ = 4
TOK = 128
HALF = 64
D = 2560
HID = 384
ROWS = NY * CAP
NC = 512
PACK = 640
STEPS = D // NC
F32 = jnp.float32
BF16 = jnp.bfloat16
NT = (((1,), (1,)), ((), ()))
N_COPIES = 115
LAST_PARTS = 2


def body(
    hand,
    grad,
    parked,
    ids_f,
    gates_f,
    ids_b,
    gates_b,
    w_gate,
    w_up,
    w_down,
    out,
    wg,
    wu,
    wd,
    ids,
    pos_rows,
    gate_rows,
    pos_cols,
    gate_cols,
    x_s,
    x_r,
    x_f,
    in_s,
    in_r,
    in_f,
    stage,
    ret_b,
    ret_f,
    far,
    near,
    hop1,
    hop2,
    own_sum,
    acc_a,
    acc_u,
    acc_q,
    act_a,
    act_u,
    p_mat,
    q_mat,
    send_sem,
    recv_sem,
    local_sem,
):
    s = lax.axis_index("section")
    e = lax.axis_index("expert")
    y = e // NZ
    z = e % NZ
    zl = s // 8
    pair = z // 2

    def at(section, yy, zz):
        return (section, yy * NZ + zz)

    zp, zm, z2 = (z + 1) % 4, (z + 3) % 4, (z + 2) % 4
    nxt, prv, mate = (s + 1) % 16, (s + 15) % 16, (s + 8) % 16
    up_to = (z + zl) % 4
    down_to = (z + 3 + zl) % 4
    zp_dev, zm_dev, z2_dev = at(s, y, zp), at(s, y, zm), at(s, y, z2)
    y_dev = [None] + [at(s, (y + r) % 4, z) for r in (1, 2, 3)]

    counter = [0]
    pending = []

    def remote(src, dst, device):
        i = counter[0]
        counter[0] += 1
        copy = pltpu.make_async_remote_copy(
            src_ref=src,
            dst_ref=dst,
            send_sem=send_sem.at[i],
            recv_sem=recv_sem.at[i],
            device_id=device,
            device_id_type=pl.DeviceIdType.MESH,
        )
        pending.append(copy)
        return copy

    local = [
        pltpu.make_async_copy(w_gate.at[0, 0], wg, local_sem.at[0]),
        pltpu.make_async_copy(w_up.at[0, 0], wu, local_sem.at[1]),
        pltpu.make_async_copy(w_down.at[0, 0], wd, local_sem.at[2]),
    ]
    for copy in local:
        copy.start()
    ids[z, 0:2, :] = ids_f[...].astype(F32)
    ids[z, 2:4, :] = gates_f[...]
    ids[z, 4:6, :] = ids_b[...].astype(F32)
    ids[z, 6:8, :] = gates_b[...]

    lower = lax.broadcasted_iota(jnp.int32, (TOK, TOK), 0) < lax.broadcasted_iota(
        jnp.int32, (TOK, TOK), 1
    )
    lower = lower.astype(F32).astype(BF16)
    expert_row = lax.broadcasted_iota(jnp.int32, (EXPERTS, TOK), 0).astype(F32)
    filler = jnp.zeros((TOK - EXPERTS, TOK), F32)

    def tables(zz):
        for which in range(2):
            base = 4 * which
            one = ids[zz, base : base + 1, :]
            two = ids[zz, base + 1 : base + 2, :]
            first = one == expert_row
            second = two == expert_row
            named = jnp.where(first | second, 1.0, 0.0)
            before = jnp.dot(named.astype(BF16), lower, preferred_element_type=F32)
            place = jnp.where(named > 0.5, before, -1.0)
            gate = jnp.where(first, ids[zz, base + 2 : base + 3, :], 0.0) + jnp.where(
                second, ids[zz, base + 3 : base + 4, :], 0.0
            )
            pos_rows[which, zz] = place
            gate_rows[which, zz] = gate
            pos_cols[which, zz] = jnp.concatenate([place, filler], axis=0).T
            gate_cols[which, zz] = jnp.concatenate([gate, filler], axis=0).T

    barrier = pltpu.get_barrier_semaphore()
    others = [at(nxt, y, z), at(prv, y, z), at(mate, y, up_to), at(mate, y, down_to)]
    others += [zp_dev, zm_dev, z2_dev] + y_dev[1:]
    for device in others:
        pl.semaphore_signal(barrier, inc=1, device_id=device, device_id_type=pl.DeviceIdType.MESH)
    tables(z)
    pl.semaphore_wait(barrier, len(others))

    meta_copies = [remote(ids.at[z], ids.at[z], device) for device in (zp_dev, zm_dev, z2_dev)]
    for copy in meta_copies:
        copy.start()
    halves = (pl.ds(0, HALF), pl.ds(HALF, HALF))
    s_up = [remote(parked.at[0, h], x_s.at[z, h], at(mate, y, up_to)) for h in halves]
    s_down = [remote(parked.at[0, h], x_s.at[z, h], at(mate, y, down_to)) for h in halves]
    wide = (pl.ds(0, D // 2), pl.ds(D // 2, D // 2))
    shift = [
        [remote(hand.at[0, :, c], x_f.at[z, :, c], at(nxt, y, z)) for c in wide],
        [remote(grad.at[0, :, c], x_r.at[z, :, c], at(prv, y, z)) for c in wide],
    ]
    for i in range(2):
        shift[1][i].start()
        shift[0][i].start()
    for one, two in zip(s_up, s_down):
        one.start()
        two.start()

    experts = [((y + r) % 4) * 2 + pair for r in range(NY)]
    slot_row = lax.broadcasted_iota(jnp.int32, (CAP, TOK), 0).astype(F32)
    own_rows = pl.ds(pl.multiple_of(y * CAP, 16), CAP)

    def columns(i):
        return pl.ds(pl.multiple_of(i * NC, NC), NC)

    def sort_rows(which, zz, source, target, slot, scaled):
        picks = []
        gates = []
        for r in range(NY):
            one = jnp.where(slot_row == pos_rows[which, zz, pl.ds(experts[r], 1), :], 1.0, 0.0)
            picks.append(one)
            if scaled:
                gates.append(
                    jnp.sum(one * gate_rows[which, zz, pl.ds(experts[r], 1), :], axis=1, keepdims=True)
                )
        p_mat[...] = jnp.concatenate(picks, axis=0).astype(BF16)
        gate = jnp.concatenate(gates, axis=0) if scaled else None

        def some(first, last):
            @pl.loop(first, last)
            def _(i):
                c = pl.ds(pl.multiple_of(i * PACK, PACK), PACK)
                rows = jnp.dot(p_mat[...], source[zz, :, c], preferred_element_type=F32)
                if scaled:
                    rows = rows * gate
                rows = rows.astype(BF16)
                target[zz, own_rows, c] = rows[:CAP]
                stage[slot, :, c] = rows[CAP:]

        return some

    def along_y(zz, target, slot, c):
        return [
            remote(
                stage.at[slot, pl.ds((r - 1) * CAP, CAP), c],
                target.at[zz, own_rows, c],
                y_dev[r],
            )
            for r in (1, 2, 3)
        ]

    def pack(which, zz, source, target, slot, scaled):
        sort_rows(which, zz, source, target, slot, scaled)(0, D // PACK)
        copies = along_y(zz, target, slot, pl.ds(0, D))
        for copy in copies:
            copy.start()
        return copies

    def forward(zz):
        acc_a[...] = jnp.zeros_like(acc_a)
        acc_u[...] = jnp.zeros_like(acc_u)

        @pl.loop(0, STEPS)
        def _(i):
            c = columns(i)
            rows = in_f[zz, :, c]
            acc_a[...] += jnp.dot(rows, wg[c, :], preferred_element_type=F32)
            acc_u[...] += jnp.dot(rows, wu[c, :], preferred_element_type=F32)

        a = acc_a[...]
        act_a[...] = (a / (1.0 + jnp.exp(-a)) * acc_u[...]).astype(BF16)

        @pl.loop(0, STEPS)
        def _(i):
            c = columns(i)
            in_f[zz, :, c] = jnp.dot(act_a[...], wd[:, c], preferred_element_type=F32).astype(BF16)

    def backward(zz):
        acc_a[...] = jnp.zeros_like(acc_a)
        acc_u[...] = jnp.zeros_like(acc_u)
        acc_q[...] = jnp.zeros_like(acc_q)

        @pl.loop(0, STEPS)
        def _(i):
            c = columns(i)
            rows = in_s[zz, :, c]
            acc_a[...] += jnp.dot(rows, wg[c, :], preferred_element_type=F32)
            acc_u[...] += jnp.dot(rows, wu[c, :], preferred_element_type=F32)
            acc_q[...] += lax.dot_general(in_r[zz, :, c], wd[:, c], NT, preferred_element_type=F32)

        a = acc_a[...]
        q = acc_q[...]
        sigma = 1.0 / (1.0 + jnp.exp(-a))
        act_a[...] = (q * acc_u[...] * sigma * (1.0 + a * (1.0 - sigma))).astype(BF16)
        act_u[...] = (q * a * sigma).astype(BF16)

        @pl.loop(0, STEPS)
        def _(i):
            c = columns(i)
            back = lax.dot_general(act_a[...], wg[c, :], NT, preferred_element_type=F32)
            back += lax.dot_general(act_u[...], wu[c, :], NT, preferred_element_type=F32)
            in_r[zz, :, c] = back.astype(BF16)

    def send_back(zz, result, returned, c=pl.ds(0, D)):
        copies = []
        for r in (1, 2, 3):
            rows = pl.ds(pl.multiple_of(((y + r) % 4) * CAP, 16), CAP)
            copy = remote(
                result.at[zz, rows, c], returned.at[zz, pl.ds((4 - r) * CAP, CAP), c], y_dev[r]
            )
            copy.start()
            copies.append(copy)
        returned[zz, pl.ds(0, CAP), c] = result[zz, own_rows, c]
        return copies

    lane = lax.broadcasted_iota(jnp.int32, (TOK, ROWS), 1)
    block = jnp.where(lane >= CAP, 1, 0) + jnp.where(lane >= 2 * CAP, 1, 0)
    block = block + jnp.where(lane >= 3 * CAP, 1, 0)
    slot_col = (lane - block * CAP).astype(F32)
    expert_lane = lax.broadcasted_iota(jnp.int32, (TOK, TOK), 1)

    def spread(table, which, zz):
        cols = table[which, zz]
        wide = jnp.zeros((TOK, ROWS), F32)
        for r in range(NY):
            one = jnp.sum(jnp.where(expert_lane == experts[r], cols, 0.0), axis=1, keepdims=True)
            wide = wide + jnp.where(block == r, one, 0.0)
        return wide

    def combine(which, zz, returned, store, first=0, last=D // PACK):
        weight = jnp.where(spread(pos_cols, which, zz) == slot_col, 1.0, 0.0)
        if which == 0:
            weight = weight * spread(gate_cols, which, zz)
            high = weight.astype(BF16)
            p_low = (weight - high.astype(F32)).astype(BF16)
            q_mat[0] = high
            q_mat[1] = p_low
        else:
            q_mat[0] = weight.astype(BF16)

        @pl.loop(first, last)
        def _(i):
            c = pl.ds(pl.multiple_of(i * PACK, PACK), PACK)
            total = jnp.dot(q_mat[0], returned[zz, :, c], preferred_element_type=F32)
            if which == 0:
                total += jnp.dot(q_mat[1], returned[zz, :, c], preferred_element_type=F32)
            store(c, total)

    def landed(copies):
        for copy in copies:
            copy.wait_recv()

    def to_far(which, returned):
        def store(c, total):
            far[which, :, c] = total.astype(BF16)

        combine(which, z2, returned, store)
        up = remote(far.at[which, halves[0]], hop1.at[which, 0], zp_dev)
        down = remote(far.at[which, halves[1]], hop1.at[which, 1], zm_dev)
        up.start()
        down.start()
        return up, down

    def to_near(which, returned, direction, arriving, back, part=0, parts=1):
        zz = zp if direction == 0 else zm
        device = zp_dev if direction == 0 else zm_dev
        through, free = halves[direction], halves[1 - direction]

        def store(c, total):
            near[which, direction, :, c] = total.astype(BF16)

        landed(back)
        steps = D // PACK // parts
        c = pl.ds(part * steps * PACK, steps * PACK)
        combine(which, zz, returned, store, part * steps, (part + 1) * steps)
        first = remote(
            near.at[which, direction, free, c], hop2.at[which, direction, free, c], device
        )
        first.start()
        if part == 0:
            arriving.wait_recv()
        near[which, direction, through, c] = (
            near[which, direction, through, c].astype(F32)
            + hop1[which, direction, :, c].astype(F32)
        ).astype(BF16)
        second = remote(
            near.at[which, direction, through, c], hop2.at[which, direction, through, c], device
        )
        second.start()
        return [first, second]

    def to_own(which, returned):
        def store(c, total):
            own_sum[which, :, c] = total

        combine(which, z, returned, store)

    def finish(which, out):
        out[which] = (
            own_sum[which] + hop2[which, 0].astype(F32) + hop2[which, 1].astype(F32)
        ).astype(BF16)

    def spread_first(x, through):
        one, two = (halves[0], halves[1]) if through else (halves[1], halves[0])
        return [
            remote(x.at[z, one], x.at[z, one], zp_dev),
            remote(x.at[z, two], x.at[z, two], zm_dev),
        ]

    def spread_second(x):
        return [
            remote(x.at[zm, halves[0]], x.at[zm, halves[0]], zp_dev),
            remote(x.at[zp, halves[1]], x.at[zp, halves[1]], zm_dev),
        ]

    def nearby(copies):
        copies[0].wait_recv()
        copies[2].wait_recv()

    def straight(copies):
        copies[1].wait_recv()

    def start(copies):
        for copy in copies:
            copy.start()

    strips = [pl.ds(i * D // LAST_PARTS, D // LAST_PARTS) for i in range(LAST_PARTS)]

    zs_up, zs_down = (z + 3 + zl) % 4, (z + zl) % 4
    zs_up2, zs_down2 = (z + 2 + zl) % 4, (z + 1 + zl) % 4

    own = [
        [along_y(z, in_f, 0, c) for c in wide],
        [along_y(z, in_r, 1, c) for c in wide],
    ]
    got_f_own, got_r_own = own[0][0] + own[0][1], own[1][0] + own[1][1]

    def own_rows_out(which):
        some = sort_rows(which, z, (x_f, x_r)[which], (in_f, in_r)[which], which, which == 1)
        for i in range(2):
            shift[which][i].wait_recv()
            some(i * D // PACK // 2, (i + 1) * D // PACK // 2)
            start(own[which][i])

    s_up2 = [remote(x_s.at[zs_up, h], x_s.at[zs_up, h], zp_dev) for h in halves]
    s_down2 = [remote(x_s.at[zs_down, h], x_s.at[zs_down, h], zm_dev) for h in halves]

    odd = s % 2 == 1

    @pl.when(odd)
    def _():
        own_rows_out(0)

    @pl.when(jnp.logical_not(odd))
    def _():
        own_rows_out(1)

    for copy in meta_copies:
        copy.wait_recv()
    for zz in (zp, zm, z2):
        tables(zz)

    for i in range(2):
        s_up[i].wait_recv()
        s_up2[i].start()
        s_down[i].wait_recv()
        s_down2[i].start()

    @pl.when(odd)
    def _():
        own_rows_out(1)

    @pl.when(jnp.logical_not(odd))
    def _():
        own_rows_out(0)

    got_s = [pack(1, zs_up, x_s, in_s, 2, False), pack(1, zs_down, x_s, in_s, 3, False)]
    for copy in local:
        copy.wait()

    r_first_a, r_first_b = spread_first(x_r, True), spread_first(x_r, False)
    f_first_a, f_first_b = spread_first(x_f, True), spread_first(x_f, False)
    r_second, f_second = spread_second(x_r), spread_second(x_f)

    landed([s_up2[0], s_down2[0]])
    start(r_first_a)
    landed(got_f_own)
    forward(z)
    landed([s_up2[1], s_down2[1]])
    start(r_first_b)
    got_s.append(pack(1, zs_up2, x_s, in_s, 4, False))
    got_s.append(pack(1, zs_down2, x_s, in_s, 5, False))
    fore_own = send_back(z, in_f, ret_f)

    landed(r_first_a)
    start(r_second)
    landed(r_first_b)
    start(f_first_a)
    got_r_p = pack(1, zp, x_r, in_r, 6, True)
    got_r_m = pack(1, zm, x_r, in_r, 7, True)
    landed(got_r_own)
    for copies in got_s:
        landed(copies)
    backward(z)
    landed(r_second)
    start(f_first_b)
    got_r_2 = pack(1, z2, x_r, in_r, 8, True)
    landed(got_r_p)
    backward(zp)
    back_p = send_back(zp, in_r, ret_b)
    landed(f_first_a)
    start(f_second)
    landed(got_r_2)
    backward(z2)
    back_2 = send_back(z2, in_r, ret_b)
    landed(got_r_m)
    backward(zm)
    landed(f_first_b)
    nearby(back_2)
    back_m = send_back(zm, in_r, ret_b)
    straight(back_2)
    b_up, b_down = to_far(1, ret_b)
    landed(f_second)
    got_f_2 = pack(0, z2, x_f, in_f, 9, False)
    b_near = to_near(1, ret_b, 0, b_up, back_p)
    got_f_p = pack(0, zp, x_f, in_f, 10, False)
    b_near += to_near(1, ret_b, 1, b_down, back_m)
    landed(got_f_2)
    forward(z2)
    fore_2 = send_back(z2, in_f, ret_f)
    got_f_m = pack(0, zm, x_f, in_f, 11, False)
    landed(got_f_p)
    forward(zp)
    nearby(fore_2)
    fore_p = [send_back(zp, in_f, ret_f, strips[0])]
    straight(fore_2)
    f_up, f_down = to_far(0, ret_f)
    landed(got_f_m)
    forward(zm)
    fore_m = [send_back(zm, in_f, ret_f, strips[0])]
    for c in strips[1:]:
        fore_p.append(send_back(zp, in_f, ret_f, c))
        fore_m.append(send_back(zm, in_f, ret_f, c))
    landed(fore_own)
    to_own(0, ret_f)
    f_near = []
    for i in range(LAST_PARTS):
        f_near += to_near(0, ret_f, 0, f_up, fore_p[i], i, LAST_PARTS)
        f_near += to_near(0, ret_f, 1, f_down, fore_m[i], i, LAST_PARTS)
        if i == 0:
            back_own = send_back(z, in_r, ret_b)
    landed(back_own)
    to_own(1, ret_b)
    landed(b_near)
    finish(1, out)
    landed(f_near)
    finish(0, out)

    for copy in pending:
        copy.wait_send()
    assert counter[0] == N_COPIES, counter[0]


def part_ways(both, out_f, out_b):
    out_f[0] = both[0]
    out_b[0] = both[1]


def on_device(
    handoff, grad_handoff, parked, ids_fwd, gates_fwd, ids_bwd, gates_bwd, w_gate, w_up, w_down
):
    meta = [ids_fwd[0].T, gates_fwd[0].T, ids_bwd[0].T, gates_bwd[0].T]
    anywhere = pl.BlockSpec(memory_space=pl.ANY)
    vmem = pl.BlockSpec(memory_space=pltpu.VMEM)
    both = pl.pallas_call(
        body,
        out_shape=jax.ShapeDtypeStruct((2, TOK, D), BF16),
        in_specs=[anywhere] * 3 + [vmem] * 4 + [anywhere] * 3,
        out_specs=vmem,
        scratch_shapes=[
            pltpu.VMEM((D, HID), BF16),
            pltpu.VMEM((D, HID), BF16),
            pltpu.VMEM((HID, D), BF16),
            pltpu.VMEM((NZ, 8, TOK), F32),
            pltpu.VMEM((2, NZ, EXPERTS, TOK), F32),
            pltpu.VMEM((2, NZ, EXPERTS, TOK), F32),
            pltpu.VMEM((2, NZ, TOK, TOK), F32),
            pltpu.VMEM((2, NZ, TOK, TOK), F32),
            pltpu.VMEM((NZ, TOK, D), BF16),
            pltpu.VMEM((NZ, TOK, D), BF16),
            pltpu.VMEM((NZ, TOK, D), BF16),
            pltpu.VMEM((NZ, ROWS, D), BF16),
            pltpu.VMEM((NZ, ROWS, D), BF16),
            pltpu.VMEM((NZ, ROWS, D), BF16),
            pltpu.VMEM((12, ROWS - CAP, D), BF16),
            pltpu.VMEM((NZ, ROWS, D), BF16),
            pltpu.VMEM((NZ, ROWS, D), BF16),
            pltpu.VMEM((2, TOK, D), BF16),
            pltpu.VMEM((2, 2, TOK, D), BF16),
            pltpu.VMEM((2, 2, HALF, D), BF16),
            pltpu.VMEM((2, 2, TOK, D), BF16),
            pltpu.VMEM((2, TOK, D), F32),
            pltpu.VMEM((ROWS, HID), F32),
            pltpu.VMEM((ROWS, HID), F32),
            pltpu.VMEM((ROWS, HID), F32),
            pltpu.VMEM((ROWS, HID), BF16),
            pltpu.VMEM((ROWS, HID), BF16),
            pltpu.VMEM((ROWS, TOK), BF16),
            pltpu.VMEM((2, TOK, ROWS), BF16),
            pltpu.SemaphoreType.DMA((N_COPIES,)),
            pltpu.SemaphoreType.DMA((N_COPIES,)),
            pltpu.SemaphoreType.DMA((3,)),
        ],
        compiler_params=pltpu.CompilerParams(
            collective_id=0, has_side_effects=True, vmem_limit_bytes=62 * 2**20
        ),
        name="relay_experts",
    )(handoff, grad_handoff, parked, *meta, w_gate, w_up, w_down)

    result = jax.ShapeDtypeStruct((1, TOK, D), BF16)
    return pl.pallas_call(
        part_ways,
        out_shape=(result, result),
        in_specs=[vmem],
        out_specs=(vmem, vmem),
        name="part_ways",
    )(both)


def solution(mesh):
    rows = P("section", "expert", None)
    weights = P("section", "expert", None, None)
    return jax.shard_map(
        on_device,
        mesh=mesh,
        in_specs=(rows,) * 7 + (weights,) * 3,
        out_specs=(rows, rows),
        check_vma=False,
    )
```
